32 devices in a mesh: ctx: 8 (over z, x), kvh: 4 (over y, core).
Axes of the slice: x: 2, y: 2, z: 4, core: 2. Of those that a mesh axis runs over, the one named last changes fastest.
Arguments:
- queries: bfloat16 [12, 16, 8192], P(None, None, 'kvh'), may hold values from -100 to 100
- keys: bfloat16 [512, 8, 256, 128], P('ctx', 'kvh'), may hold values from -8 to 8
- values: bfloat16 [512, 8, 256, 128], P('ctx', 'kvh'), may hold values from -6 to 6
- out_weight: bfloat16 [8192, 8192], P('kvh', 'ctx'), may hold values from -0.0625 to 0.0625
- lengths: int32 [12], replicated, may hold values from 16 to 16384, as said below
- slot_request: int32 [512], P('ctx'), may hold values from 0 to 12, as said below
- slot_page: int32 [512], P('ctx'), may hold values from 0 to 63, as said below
Outputs:
- projected: bfloat16 [192, 8192], P('kvh', 'ctx')
The draws below stay inside these ranges and needn't reach their ends.
Inputs may be any that keep to these rules, and one draw needn't show every extreme that they name: `lengths`: some request has length 16 and some request has length 16384. slot_request is 12 for an empty slot; each page 0 to (lengths[r] - 1) // 256 of request r stands in exactly one slot, and no other page of it does. `slot_page`: 0 for an empty slot.
All inputs are finite; a program needn't handle non-finite values.
Results may differ from the reference program's by a relative error of at most 0.015.
Values may be sent and summed in bfloat16 or wider, within the bound.
No kernel may reach another device: no remote copies, remote signals or barrier semaphores. Data moves between devices by JAX's collectives and lax.ppermute only.
A program may use at most 128 MiB of HBM per device.

```python
import math
import jax
import jax.numpy as jnp
from jax import lax

D = 8192
QUERY_HEADS = 64
KEY_VALUE_HEADS = 8
HEAD_SIZE = 128
REQUEST_COUNT = 12
DRAFT_TOKENS = 16
PAGE_TOKENS = 256
PAGES_DEV = 64
PAGE_SLOTS = 512
N_CTX = 8


def layout(key):
    base = jax.random.fold_in(key, 7001)
    parts = jax.random.split(base, 6)
    slot_ids = jnp.arange(PAGE_SLOTS, dtype=jnp.int32)
    device_ids = jnp.arange(N_CTX, dtype=jnp.int32)
    fullest = jax.random.randint(parts[0], (), 0, N_CTX)
    powers = jax.random.randint(parts[1], (N_CTX,), 0, 4)
    powers = jnp.where(device_ids == fullest, 3, powers)
    live_count = jnp.array([1, 2, 4, 8], dtype=jnp.int32)[powers] * PAGES_DEV // 8
    owner_dev = slot_ids // PAGES_DEV
    live = slot_ids % PAGES_DEV < live_count[owner_dev]
    live_total = jnp.sum(live_count)
    request_ids = jnp.arange(REQUEST_COUNT, dtype=jnp.int32)
    heaviest = jax.random.randint(parts[2], (), 0, REQUEST_COUNT)
    lightest = (heaviest + 1) % REQUEST_COUNT
    others = (request_ids != heaviest) & (request_ids != lightest)
    shares = jax.random.randint(parts[3], (REQUEST_COUNT,), 1, 25)
    shares = jnp.where(others, shares, 0)
    spare = live_total - REQUEST_COUNT - PAGES_DEV
    extra = shares * spare // jnp.maximum(jnp.sum(shares), 1)
    counts = jnp.minimum(extra + 1, PAGES_DEV)
    counts = jnp.where(request_ids == heaviest, PAGES_DEV, counts)
    counts = jnp.where(request_ids == lightest, 1, counts)
    starts = jnp.cumsum(counts) - counts
    used = jnp.sum(counts)
    priority = jnp.where(live, jax.random.permutation(parts[4], PAGE_SLOTS).astype(jnp.int32), PAGE_SLOTS + slot_ids)
    ranks = jnp.argsort(jnp.argsort(priority)).astype(jnp.int32)
    holds = ranks < used
    owner_req = jnp.sum((starts[None, :] <= ranks[:, None]).astype(jnp.int32), axis=1) - 1
    owner_safe = jnp.clip(owner_req, 0, REQUEST_COUNT - 1)
    slot_request = jnp.where(holds, owner_req, REQUEST_COUNT).astype(jnp.int32)
    slot_page = jnp.where(holds, ranks - starts[owner_safe], 0).astype(jnp.int32)
    tails = jax.random.randint(parts[5], (REQUEST_COUNT,), DRAFT_TOKENS, PAGE_TOKENS + 1)
    tails = jnp.where(request_ids == heaviest, PAGE_TOKENS, tails)
    tails = jnp.where(request_ids == lightest, DRAFT_TOKENS, tails)
    lengths = ((counts - 1) * PAGE_TOKENS + tails).astype(jnp.int32)
    return (lengths, slot_request, slot_page)


def draw_lengths(key, part):
    return layout(key)[0]


def draw_slot_request(key, part):
    return layout(key)[1]


def draw_slot_page(key, part):
    return layout(key)[2]


def draw_keys(key, part):
    random_noise_key = jax.random.fold_in(key, 9201)
    return jnp.clip(jax.random.normal(random_noise_key, (PAGE_SLOTS, KEY_VALUE_HEADS, PAGE_TOKENS, HEAD_SIZE), jnp.float32), -6.0, 6.0).astype(jnp.bfloat16)


def draw_queries(key, part):
    streams = jax.random.split(jax.random.fold_in(key, 9301), 2)
    head_scale = jnp.exp(jax.random.uniform(streams[0], (QUERY_HEADS,), jnp.float32, math.log(0.5), math.log(20.0)))
    head_scale = jnp.repeat(head_scale, HEAD_SIZE)
    normal_part = jnp.clip(jax.random.normal(streams[1], (REQUEST_COUNT, DRAFT_TOKENS, QUERY_HEADS * HEAD_SIZE), jnp.float32), -6.0, 6.0)
    return jnp.clip(normal_part * head_scale, -100.0, 100.0).astype(jnp.bfloat16)


def level_of(stream_key, shape, pieces, low, top_value):
    def one(axis_at, blocks):
        draws = jax.random.uniform(jax.random.fold_in(jax.random.fold_in(stream_key, 6), axis_at), (blocks,), jnp.float32, low / len(pieces), top_value / len(pieces))
        return jnp.repeat(jnp.exp(draws), shape[axis_at] // blocks).reshape((-1,) + (1,) * (len(shape) - axis_at - 1))

    factor_of = one(*pieces[0])
    for cut in pieces[1:]:
        factor_of = factor_of * one(*cut)
    return factor_of


def gaussian(own_key, shape, deviation, reach, shards=(), kind=jnp.bfloat16):
    result = jax.random.normal(own_key, shape, jnp.float32) * deviation
    if len(shards) > 0:
        result = level_of(own_key, shape, shards, -0.22, 0.18) * result
    return jnp.clip(result, min=-reach, max=reach).astype(kind)


def setup_inputs(seed: int = 0) -> dict:
    key_of = jax.random.split(jax.random.key(seed), 8)
    queries = draw_queries(jax.random.fold_in(key_of[7], 71), 0)
    keys = draw_keys(jax.random.fold_in(key_of[7], 71), 0)
    values = gaussian(key_of[2], (PAGE_SLOTS, KEY_VALUE_HEADS, PAGE_TOKENS, HEAD_SIZE), 1.0, 6.0, ((0, 8), (1, 4)))
    out_weight = gaussian(key_of[3], (QUERY_HEADS * HEAD_SIZE, D), (QUERY_HEADS * HEAD_SIZE) ** -0.5, 0.0625, ((0, 4), (1, 8)))
    lengths = draw_lengths(jax.random.fold_in(key_of[7], 71), 0)
    slot_request = draw_slot_request(jax.random.fold_in(key_of[7], 71), 0)
    slot_page = draw_slot_page(jax.random.fold_in(key_of[7], 71), 0)
    return {"queries": queries, "keys": keys, "values": values, "out_weight": out_weight, "lengths": lengths, "slot_request": slot_request, "slot_page": slot_page}


NEGATIVE_FLOOR = -1e+30
PRECISE = lax.Precision.HIGHEST

def reference(queries, keys, values, out_weight, lengths, slot_request, slot_page):
    query_group_width = QUERY_HEADS // KEY_VALUE_HEADS
    query_matrix_rows = DRAFT_TOKENS * query_group_width
    score_scale = 1.0 / math.sqrt(HEAD_SIZE)
    query_lookup_table = queries.reshape(REQUEST_COUNT, DRAFT_TOKENS, KEY_VALUE_HEADS, query_group_width, HEAD_SIZE).transpose(0, 2, 1, 3, 4).reshape(REQUEST_COUNT, KEY_VALUE_HEADS, query_matrix_rows, HEAD_SIZE).astype(jnp.float32)
    pages_per_block = 8
    block_total = keys.shape[0] // pages_per_block
    key_cache_blocks = keys.reshape(block_total, pages_per_block, KEY_VALUE_HEADS, PAGE_TOKENS, HEAD_SIZE)
    value_cache_blocks = values.reshape(block_total, pages_per_block, KEY_VALUE_HEADS, PAGE_TOKENS, HEAD_SIZE)
    request_blocks = slot_request.reshape(block_total, pages_per_block)
    index_blocks = slot_page.reshape(block_total, pages_per_block)
    draft_row = jnp.arange(query_matrix_rows, dtype=jnp.int32) // query_group_width
    token_index = jnp.arange(PAGE_TOKENS, dtype=jnp.int32)
    request_ids = jnp.arange(REQUEST_COUNT, dtype=jnp.int32)

    def visit(running, block_data):
        maxima, running_totals, output_rows = running
        key_block, value_block, page_request, page_index = block_data
        belongs = page_request[:, None] == request_ids[None, :]
        onehot = belongs.astype(jnp.float32)
        chosen = jnp.einsum('br,rhqd->bhqd', onehot, query_lookup_table, precision=PRECISE)
        scores = jnp.einsum('bhqd,bhkd->bhqk', chosen, key_block.astype(jnp.float32), precision=PRECISE) * score_scale
        own_length = lax.optimization_barrier(jnp.sum(jnp.where(belongs, lengths[None, :], 0), axis=1))
        query_pos = own_length[:, None] - DRAFT_TOKENS + draft_row[None, :]
        key_pos = page_index[:, None] * PAGE_TOKENS + token_index[None, :]
        visible = (page_request < REQUEST_COUNT)[:, None, None] & (key_pos[:, None, :] <= query_pos[:, :, None])
        visible = visible[:, None, :, :]
        masked = jnp.where(visible, scores, NEGATIVE_FLOOR)
        page_max = lax.optimization_barrier(jnp.max(masked, axis=3))
        weights = jnp.where(visible, jnp.exp(masked - page_max[..., None]), 0.0)
        page_mass = lax.optimization_barrier(jnp.sum(weights, axis=3))
        rounded = lax.optimization_barrier(weights.astype(jnp.bfloat16)).astype(jnp.float32)
        page_out = jnp.einsum('bhqk,bhkd->bhqd', rounded, value_block.astype(jnp.float32), precision=PRECISE)
        request_max = lax.optimization_barrier(jnp.max(jnp.where(belongs[:, :, None, None], page_max[:, None], NEGATIVE_FLOOR), axis=0))
        new_maxima = jnp.maximum(maxima, request_max)
        carry_keep = jnp.exp(maxima - new_maxima)
        page_ref = jnp.einsum('br,rhq->bhq', onehot, new_maxima, precision=PRECISE)
        factor = jnp.exp(page_max - page_ref)
        running_totals = running_totals * carry_keep + jnp.einsum('br,bhq->rhq', onehot, page_mass * factor, precision=PRECISE)
        output_rows = output_rows * carry_keep[..., None] + jnp.einsum('br,bhqd->rhqd', onehot, page_out * factor[..., None], precision=PRECISE)
        return ((new_maxima, running_totals, output_rows), None)
    initial_state = (jnp.full((REQUEST_COUNT, KEY_VALUE_HEADS, query_matrix_rows), NEGATIVE_FLOOR, jnp.float32), jnp.zeros((REQUEST_COUNT, KEY_VALUE_HEADS, query_matrix_rows), jnp.float32), jnp.zeros((REQUEST_COUNT, KEY_VALUE_HEADS, query_matrix_rows, HEAD_SIZE), jnp.float32))
    (maxima, running_totals, output_rows), unused = lax.scan(visit, initial_state, (key_cache_blocks, value_cache_blocks, request_blocks, index_blocks))
    attended_output = (output_rows / running_totals[..., None]).reshape(REQUEST_COUNT, KEY_VALUE_HEADS, DRAFT_TOKENS, query_group_width, HEAD_SIZE).transpose(0, 2, 1, 3, 4).reshape(REQUEST_COUNT * DRAFT_TOKENS, QUERY_HEADS * HEAD_SIZE).astype(jnp.bfloat16)
    return jnp.dot(attended_output, out_weight, preferred_element_type=jnp.float32).astype(jnp.bfloat16)
```

```python
import functools
import math

import jax
import jax.numpy as jnp
from jax import lax
from jax.experimental import pallas as pl
from jax.experimental.pallas import tpu as pltpu
from jax.sharding import PartitionSpec as P

QUERY_HEADS = 64
KEY_VALUE_HEADS = 8
GROUP = QUERY_HEADS // KEY_VALUE_HEADS
DRAFT = 16
FLOOR = -1e30
LANES = 128
CHUNK = 4
UNROLL = 2


def attention_kernel(
    n_ctx, hps, tg,
    len_ref, req_ref, page_ref, q_ref, k_hbm, v_hbm, *rest,
):
    msgs = rest[:n_ctx]
    k_buf, v_buf, acc, top, mass, sems = rest[n_ctx:]
    slots, kv_local, page_len, head = k_hbm.shape
    requests = q_ref.shape[0]
    chunks = slots // CHUNK
    rows = GROUP * DRAFT
    scale = math.log2(math.e) / math.sqrt(head)

    def copies(i):
        at = pl.ds(i * CHUNK, CHUNK)
        return (
            pltpu.make_async_copy(k_hbm.at[at], k_buf.at[at], sems.at[0, i]),
            pltpu.make_async_copy(v_hbm.at[at], v_buf.at[at], sems.at[1, i]),
        )

    @pl.loop(0, chunks)
    def _(i):
        for copy in copies(i):
            copy.start()

    @pl.loop(0, requests)
    def _(r):
        top[r] = jnp.full(top.shape[1:], FLOOR, jnp.float32)
        mass[r] = jnp.zeros(mass.shape[1:], jnp.float32)
        acc[r] = jnp.zeros(acc.shape[1:], jnp.float32)

    ones = jnp.ones((page_len, LANES), jnp.bfloat16)
    offset = (
        lax.broadcasted_iota(jnp.int32, (rows, page_len), 1)
        - lax.broadcasted_iota(jnp.int32, (rows, page_len), 0) % DRAFT
    )

    def step(first, masked):
        work = []
        for u in range(UNROLL):
            s = first + u
            r = req_ref[s]
            r_in = jnp.minimum(r, requests - 1)
            last = len_ref[r_in] - DRAFT - page_ref[s] * page_len
            for h in range(kv_local):
                q = jnp.concatenate(
                    [q_ref[r_in, :, pl.ds((h * GROUP + g) * head, head)] for g in range(GROUP)], axis=0
                )
                scores = lax.dot_general(
                    q, k_buf[s, h], (((1,), (1,)), ((), ())), preferred_element_type=jnp.float32
                )
                if masked:
                    scores = jnp.where(offset <= last, scores, FLOOR)
                work.append((s, r, h, scores, jnp.max(scores, axis=1, keepdims=True)))
        weighted = []
        for s, r, h, scores, high in work:
            before = top[r, h]
            after = jnp.maximum(before, high)
            top[r, h] = after
            weights = jnp.concatenate(
                [
                    jnp.exp2((scores[:, i : i + LANES] - after) * scale).astype(jnp.bfloat16)
                    for i in range(0, page_len, LANES)
                ],
                axis=1,
            )
            weighted.append((s, r, h, weights, jnp.exp2((before - after) * scale)))
        for s, r, h, weights, keep in weighted:
            both = jnp.dot(
                weights,
                jnp.concatenate([v_buf[s, h], ones], axis=1),
                preferred_element_type=jnp.float32,
            )
            acc[r, h] = acc[r, h] * keep + both[:, :head]
            mass[r, h] = mass[r, h] * keep + both[:, head:]

    @pl.loop(0, chunks)
    def _(i):
        for copy in copies(i):
            copy.wait()

        @pl.loop(0, CHUNK // UNROLL)
        def _(j):
            first = i * CHUNK + j * UNROLL
            cut = False
            for u in range(UNROLL):
                s = first + u
                r = req_ref[s]
                r_in = jnp.minimum(r, requests - 1)
                end = page_ref[s] * page_len + page_len - 1
                cut = cut | ((r < requests) & (end > len_ref[r_in] - DRAFT))

            @pl.when(cut)
            def _():
                step(first, True)

            @pl.when(jnp.logical_not(cut))
            def _():
                step(first, False)

    me = lax.axis_index("ctx")
    per = requests // tg
    width = hps * LANES
    group = width // 4
    lane = lax.broadcasted_iota(jnp.int32, (DRAFT, LANES), 1)
    for d in range(n_ctx):
        dest = me ^ d
        part = dest % tg
        first_head = dest // tg * hps
        stat = [jnp.zeros((DRAFT, LANES), jnp.float32) for _ in range(hps)]

        def put(at, value):
            stat[at // LANES] = jnp.where(lane == at % LANES, value, stat[at // LANES])

        for rr in range(per):
            r = part * per + rr
            for hh in range(hps):
                q_head = first_head + hh
                h, g = q_head // GROUP, q_head % GROUP
                at = pl.ds(g * DRAFT, DRAFT)
                m = top[r, h, at, :]
                l = mass[r, h, at, :]
                o = acc[r, h, at, :]
                msgs[d][rr * DRAFT : (rr + 1) * DRAFT, hh * LANES : (hh + 1) * LANES] = (
                    o / jnp.where(l > 0, l, 1.0)
                ).astype(jnp.bfloat16)
                m_sent = m.astype(jnp.bfloat16).astype(jnp.float32)
                l_sent = jnp.where(m > 0.5 * FLOOR, l * jnp.exp2((m - m_sent) * scale), 0.0)
                l_high = l_sent.astype(jnp.bfloat16).astype(jnp.float32)
                t = rr * hps + hh
                put(t, m_sent)
                put(group + t, l_high)
                put(2 * group + t, l_sent - l_high)
        msgs[d][per * DRAFT :, :] = jnp.concatenate(stat, axis=1).astype(jnp.bfloat16)


def combine_kernel(n_ctx, scale, *refs):
    parts, out = refs[:n_ctx], refs[n_ctx]
    rows, width = out.shape
    per, hps, group = rows // DRAFT, width // LANES, width // 4
    tops, masses = [], []
    for p in parts:
        stat = p[rows:, :].astype(jnp.float32)
        tops.append(stat[:, :group])
        masses.append(stat[:, group : 2 * group] + stat[:, 2 * group : 3 * group])
    best = functools.reduce(jnp.maximum, tops)
    shares = [l * jnp.exp2((m - best) * scale) for m, l in zip(tops, masses)]
    total = functools.reduce(jnp.add, shares)
    lanes = lax.broadcasted_iota(jnp.int32, total.shape, 1)
    inverse = 1.0 / jnp.where(lanes < per * hps, total, 1.0)
    shares = [s * inverse for s in shares]
    for rr in range(per):
        for hh in range(hps):
            t = rr * hps + hh
            at = (slice(rr * DRAFT, (rr + 1) * DRAFT), slice(hh * LANES, (hh + 1) * LANES))
            out[at] = functools.reduce(
                jnp.add,
                [s[:, t : t + 1] * p[at].astype(jnp.float32) for s, p in zip(shares, parts)],
            ).astype(jnp.bfloat16)


def project_kernel(n_ctx, n_kvh, tg, *refs):
    parts, w_ref = refs[:n_ctx], refs[n_ctx]
    outs = refs[n_ctx + 1 : n_ctx + 1 + n_kvh]
    a_buf, total = refs[n_ctx + 1 + n_kvh :]
    rows, width = parts[0].shape
    me = lax.axis_index("ctx")
    for d, p in enumerate(parts):
        source = me ^ d
        a_buf[
            pl.ds(pl.multiple_of(source % tg * rows, rows), rows),
            pl.ds(pl.multiple_of(source // tg * width, width), width),
        ] = p[...]
    total[...] = jnp.dot(a_buf[...], w_ref[...], preferred_element_type=jnp.float32)
    mine = lax.axis_index("kvh")
    count = outs[0].shape[0]
    for d, o in enumerate(outs):
        o[...] = total[pl.ds(pl.multiple_of((mine ^ d) * count, 8), count), :].astype(jnp.bfloat16)


def exchange(x, axis, d):
    return lax.ppermute(x, axis, [(i, i ^ d) for i in range(lax.axis_size(axis))])


def per_device(queries, keys, values, out_weight, lengths, slot_request, slot_page):
    n_ctx, n_kvh = lax.axis_size("ctx"), lax.axis_size("kvh")
    requests = queries.shape[0]
    slots, kv_local, page_len, head = keys.shape
    heads = kv_local * GROUP
    hps, tg = max(heads // n_ctx, 1), max(n_ctx // heads, 1)
    tokens = requests * DRAFT
    rows, width = tokens // tg, hps * head
    unit = GROUP * DRAFT
    smem = pl.BlockSpec(memory_space=pltpu.SMEM)
    vmem = pl.BlockSpec(memory_space=pltpu.VMEM)
    hbm = pl.BlockSpec(memory_space=pl.ANY)
    params = pltpu.CompilerParams(vmem_limit_bytes=48 * 2**20)
    msgs = pl.pallas_call(
        functools.partial(attention_kernel, n_ctx, hps, tg),
        out_shape=[jax.ShapeDtypeStruct((rows + DRAFT, width), jnp.bfloat16)] * n_ctx,
        in_specs=[smem, smem, smem, vmem, hbm, hbm],
        out_specs=[vmem] * n_ctx,
        scratch_shapes=[
            pltpu.VMEM(keys.shape, keys.dtype),
            pltpu.VMEM(values.shape, values.dtype),
            pltpu.VMEM((requests + 1, kv_local, unit, head), jnp.float32),
            pltpu.VMEM((requests + 1, kv_local, unit, head), jnp.float32),
            pltpu.VMEM((requests + 1, kv_local, unit, head), jnp.float32),
            pltpu.SemaphoreType.DMA((2, slots // CHUNK)),
        ],
        compiler_params=params,
    )(lengths, slot_request, slot_page, queries, keys, values)
    got = [msgs[0]] + [exchange(msgs[d], "ctx", d) for d in range(1, n_ctx)]
    scale = math.log2(math.e) / math.sqrt(head)
    attended = pl.pallas_call(
        functools.partial(combine_kernel, n_ctx, scale),
        out_shape=jax.ShapeDtypeStruct((rows, width), jnp.bfloat16),
        in_specs=[vmem] * n_ctx,
        out_specs=vmem,
        compiler_params=params,
    )(*got)
    every = [attended] + [exchange(attended, "ctx", d) for d in range(1, n_ctx)]
    columns = out_weight.shape[1]
    partial = pl.pallas_call(
        functools.partial(project_kernel, n_ctx, n_kvh, tg),
        out_shape=[jax.ShapeDtypeStruct((tokens // n_kvh, columns), jnp.bfloat16)] * n_kvh,
        in_specs=[vmem] * (n_ctx + 1),
        out_specs=[vmem] * n_kvh,
        scratch_shapes=[
            pltpu.VMEM((tokens, heads * head), jnp.bfloat16),
            pltpu.VMEM((tokens, columns), jnp.float32),
        ],
        compiler_params=params,
    )(*every, out_weight)
    sums = partial[0].astype(jnp.float32)
    for d in range(1, n_kvh):
        sums = sums + exchange(partial[d], "kvh", d).astype(jnp.float32)
    return sums.astype(jnp.bfloat16)


def solution(mesh):
    placed = (
        P(None, None, "kvh"),
        P("ctx", "kvh", None, None),
        P("ctx", "kvh", None, None),
        P("kvh", "ctx"),
        P(),
        P("ctx"),
        P("ctx"),
    )
    return jax.shard_map(
        per_device, mesh=mesh, in_specs=placed, out_specs=P("kvh", "ctx"), check_vma=False
    )
```

```python
import functools
import math

import jax
import jax.numpy as jnp
from jax import lax
from jax.experimental import pallas as pl
from jax.experimental.pallas import tpu as pltpu
from jax.sharding import PartitionSpec as P

QUERY_HEADS = 64
KEY_VALUE_HEADS = 8
GROUP = QUERY_HEADS // KEY_VALUE_HEADS
DRAFT = 16
FLOOR = -1e30
LANES = 128
CHUNK = 16
COPIES = 4


def attention_kernel(
    n_ctx, hps, tg,
    len_hbm, req_hbm, page_hbm, q_hbm, k_hbm, v_hbm, *rest,
):
    msgs = rest[:n_ctx]
    len_ref, req_ref, page_ref, q_ref, k_buf, v_buf, raw, top, acc, sems, head_sems = rest[n_ctx:]
    slots, kv_local, page_len, head = k_hbm.shape
    requests = q_ref.shape[0]
    chunks = slots // CHUNK
    rows = GROUP * DRAFT
    scale = math.log2(math.e) / math.sqrt(head)

    def load(i, which):
        size = CHUNK // COPIES
        at = pl.ds(i * size, size)
        source, target = ((k_hbm, k_buf), (v_hbm, v_buf))[which]
        return pltpu.make_async_copy(source.at[at], target.at[at], sems.at[which, i])

    def start(i, which):
        for c in range(COPIES):
            load(i * COPIES + c, which).start()

    def wait(i, which):
        for c in range(COPIES):
            load(i * COPIES + c, which).wait()

    first_loads = [
        pltpu.make_async_copy(source, target, head_sems.at[n])
        for n, (source, target) in enumerate(
            ((len_hbm, len_ref), (req_hbm, req_ref), (page_hbm, page_ref), (q_hbm, q_ref))
        )
    ]
    for copy in first_loads:
        copy.start()

    @pl.loop(0, chunks)
    def _(i):
        start(i, 0)

    @pl.loop(0, requests + 1)
    def _(r):
        top[r] = jnp.full(top.shape[1:], FLOOR, jnp.float32)
        acc[r] = jnp.zeros(acc.shape[1:], jnp.float32)

    for copy in first_loads:
        copy.wait()

    ones = jnp.ones((page_len, LANES), jnp.bfloat16)

    def score(first, masked):
        for u in range(CHUNK):
            s = first + u
            r = req_ref[s]
            r_in = jnp.minimum(r, requests - 1)
            for h in range(kv_local):
                q = jnp.concatenate(
                    [q_ref[r_in, :, pl.ds((h * GROUP + g) * head, head)] for g in range(GROUP)], axis=0
                )
                scores = lax.dot_general(
                    q, k_buf[s, h], (((1,), (1,)), ((), ())), preferred_element_type=jnp.float32
                )
                if masked:
                    last = len_ref[r_in] - DRAFT - page_ref[s] * page_len
                    offset = (
                        lax.broadcasted_iota(jnp.int32, (rows, page_len), 1)
                        - lax.broadcasted_iota(jnp.int32, (rows, page_len), 0) % DRAFT
                    )
                    scores = jnp.where(offset <= last, scores, FLOOR)
                raw[s, h] = scores
                high = functools.reduce(
                    jnp.maximum, [scores[:, i : i + LANES] for i in range(0, page_len, LANES)]
                )
                top[r, h] = jnp.maximum(top[r, h], high)

    @pl.loop(0, chunks)
    def _(i):
        start(i, 1)
        wait(i, 0)
        cut = False
        for u in range(CHUNK):
            s = i * CHUNK + u
            r = req_ref[s]
            end = page_ref[s] * page_len + page_len - 1
            cut = cut | ((r < requests) & (end > len_ref[jnp.minimum(r, requests - 1)] - DRAFT))

        @pl.when(cut)
        def _():
            score(i * CHUNK, True)

        @pl.when(jnp.logical_not(cut))
        def _():
            score(i * CHUNK, False)

    @pl.loop(0, requests)
    def _(r):
        for h in range(kv_local):
            top[r, h] = jnp.broadcast_to(
                jnp.max(top[r, h], axis=1, keepdims=True), (rows, LANES)
            )

    @pl.loop(0, chunks)
    def _(i):
        wait(i, 1)
        for u in range(CHUNK):
            s = i * CHUNK + u
            r = req_ref[s]
            for h in range(kv_local):
                high = top[r, h]
                weights = jnp.concatenate(
                    [
                        jnp.exp2((raw[s, h, :, i : i + LANES] - high) * scale).astype(jnp.bfloat16)
                        for i in range(0, page_len, LANES)
                    ],
                    axis=1,
                )
                acc[r, h] += jnp.dot(
                    weights,
                    jnp.concatenate([v_buf[s, h], ones], axis=1),
                    preferred_element_type=jnp.float32,
                )

    me = lax.axis_index("ctx")
    per = requests // tg
    width = hps * LANES
    group = width // 4
    lane = lax.broadcasted_iota(jnp.int32, (DRAFT, LANES), 1)
    for d in range(n_ctx):
        dest = me ^ d
        part = dest % tg
        first_head = dest // tg * hps
        tops = jnp.full((DRAFT, LANES), FLOOR, jnp.float32)
        sums = jnp.zeros((DRAFT, LANES), jnp.float32)
        for rr in range(per):
            r = part * per + rr
            for hh in range(hps):
                q_head = first_head + hh
                h, g = q_head // GROUP, q_head % GROUP
                at = pl.ds(g * DRAFT, DRAFT)
                m = top[r, h, at, :]
                l = acc[r, h, at, head:]
                o = acc[r, h, at, :head]
                msgs[d][rr * DRAFT : (rr + 1) * DRAFT, hh * LANES : (hh + 1) * LANES] = (
                    o * pl.reciprocal(jnp.where(l > 0, l, 1.0), approx=True)
                ).astype(jnp.bfloat16)
                t = rr * hps + hh
                tops = jnp.where(lane == t, m, tops)
                sums = jnp.where(lane == t, l, sums)
        tops_sent = tops.astype(jnp.bfloat16).astype(jnp.float32)
        sums = jnp.where(tops > 0.5 * FLOOR, sums * jnp.exp2((tops - tops_sent) * scale), 0.0)
        sums_high = sums.astype(jnp.bfloat16).astype(jnp.float32)
        msgs[d][per * DRAFT :, :] = jnp.concatenate(
            [x[:, :group] for x in (tops_sent, sums_high, sums - sums_high, sums)], axis=1
        ).astype(jnp.bfloat16)


def combine_kernel(final, scale, *refs):
    parts, out = refs[:-1], refs[-1]
    width = out.shape[1]
    rows = parts[0].shape[0] - DRAFT
    per, hps, group = rows // DRAFT, width // LANES, width // 4
    tops, masses = [], []
    for p in parts:
        stat = p[rows:, :].astype(jnp.float32)
        tops.append(stat[:, :group])
        masses.append(stat[:, group : 2 * group] + stat[:, 2 * group : 3 * group])
    best = functools.reduce(jnp.maximum, tops)
    shares = [l * jnp.exp2((m - best) * scale) for m, l in zip(tops, masses)]
    total = functools.reduce(jnp.add, shares)
    inverse = 1.0 / jnp.where(total > 0, total, 1.0)
    shares = [s * inverse for s in shares]
    for rr in range(per):
        for hh in range(hps):
            t = rr * hps + hh
            at = (slice(rr * DRAFT, (rr + 1) * DRAFT), slice(hh * LANES, (hh + 1) * LANES))
            out[at] = functools.reduce(
                jnp.add,
                [s[:, t : t + 1] * p[at].astype(jnp.float32) for s, p in zip(shares, parts)],
            ).astype(jnp.bfloat16)
    if not final:
        high = total.astype(jnp.bfloat16).astype(jnp.float32)
        out[rows:, :] = jnp.concatenate([best, high, total - high, total], axis=1).astype(jnp.bfloat16)


def project_kernel(n_ctx, n_kvh, tg, *refs):
    parts, w_ref = refs[:n_ctx], refs[n_ctx]
    outs = refs[n_ctx + 1 : n_ctx + 1 + n_kvh]
    a_buf, total = refs[n_ctx + 1 + n_kvh :]
    rows, width = parts[0].shape
    me = lax.axis_index("ctx")
    for d, p in enumerate(parts):
        source = me ^ d
        a_buf[
            pl.ds(pl.multiple_of(source % tg * rows, rows), rows),
            pl.ds(pl.multiple_of(source // tg * width, width), width),
        ] = p[...]
    total[...] = jnp.dot(a_buf[...], w_ref[...], preferred_element_type=jnp.float32)
    mine = lax.axis_index("kvh")
    count = outs[0].shape[0]
    for d, o in enumerate(outs):
        o[...] = total[pl.ds(pl.multiple_of((mine ^ d) * count, 8), count), :].astype(jnp.bfloat16)


def exchange(x, axis, d):
    return lax.ppermute(x, axis, [(i, i ^ d) for i in range(lax.axis_size(axis))])


def per_device(queries, keys, values, out_weight, lengths, slot_request, slot_page):
    n_ctx, n_kvh = lax.axis_size("ctx"), lax.axis_size("kvh")
    requests = queries.shape[0]
    slots, kv_local, page_len, head = keys.shape
    heads = kv_local * GROUP
    hps, tg = max(heads // n_ctx, 1), max(n_ctx // heads, 1)
    tokens = requests * DRAFT
    rows, width = tokens // tg, hps * head
    unit = GROUP * DRAFT
    smem = pl.BlockSpec(memory_space=pltpu.SMEM)
    vmem = pl.BlockSpec(memory_space=pltpu.VMEM)
    hbm = pl.BlockSpec(memory_space=pltpu.HBM)
    params = pltpu.CompilerParams(vmem_limit_bytes=46 * 2**20)
    small = pltpu.CompilerParams(vmem_limit_bytes=16 * 2**20)
    msgs = pl.pallas_call(
        functools.partial(attention_kernel, n_ctx, hps, tg),
        out_shape=[jax.ShapeDtypeStruct((rows + DRAFT, width), jnp.bfloat16)] * n_ctx,
        in_specs=[hbm] * 6,
        out_specs=[vmem] * n_ctx,
        scratch_shapes=[
            pltpu.SMEM(lengths.shape, jnp.int32),
            pltpu.SMEM(slot_request.shape, jnp.int32),
            pltpu.SMEM(slot_page.shape, jnp.int32),
            pltpu.VMEM(queries.shape, queries.dtype),
            pltpu.VMEM(keys.shape, keys.dtype),
            pltpu.VMEM(values.shape, values.dtype),
            pltpu.VMEM((slots, kv_local, unit, page_len), jnp.float32),
            pltpu.VMEM((requests + 1, kv_local, unit, LANES), jnp.float32),
            pltpu.VMEM((requests + 1, kv_local, unit, head + LANES), jnp.float32),
            pltpu.SemaphoreType.DMA((2, slots // CHUNK * COPIES)),
            pltpu.SemaphoreType.DMA((4,)),
        ],
        compiler_params=params,
    )(*(pltpu.with_memory_space_constraint(x, pltpu.HBM) for x in (lengths, slot_request, slot_page, queries)), keys, values)
    scale = math.log2(math.e) / math.sqrt(head)

    def combine(parts, final):
        shape = (rows if final else rows + DRAFT, width)
        return pl.pallas_call(
            functools.partial(combine_kernel, final, scale),
            out_shape=jax.ShapeDtypeStruct(shape, jnp.bfloat16),
            in_specs=[vmem] * len(parts),
            out_specs=vmem,
            compiler_params=small,
        )(*parts)

    across = sorted(range(0, n_ctx, 2), key=lambda d: (d == 0, d < 4, d))
    beside = {d: exchange(msgs[d + 1], "ctx", 1) for d in across}
    got = [exchange(combine([msgs[d], beside[d]], False), "ctx", d) for d in across[:-1]]
    attended = combine([msgs[0], beside[0], *got], True)
    every = {0: attended}
    for d in sorted(range(2, n_ctx, 2), key=lambda d: (d < 4, d)):
        every[d] = exchange(attended, "ctx", d)
    for d in sorted(range(0, n_ctx, 2), key=lambda d: (d != 0, d < 4, d)):
        every[d + 1] = exchange(every[d], "ctx", 1)
    every = [every[d] for d in range(n_ctx)]
    columns = out_weight.shape[1]
    partial = pl.pallas_call(
        functools.partial(project_kernel, n_ctx, n_kvh, tg),
        out_shape=[jax.ShapeDtypeStruct((tokens // n_kvh, columns), jnp.bfloat16)] * n_kvh,
        in_specs=[vmem] * (n_ctx + 1),
        out_specs=[vmem] * n_kvh,
        scratch_shapes=[
            pltpu.VMEM((tokens, heads * head), jnp.bfloat16),
            pltpu.VMEM((tokens, columns), jnp.float32),
        ],
        compiler_params=small,
    )(*every, out_weight)
    sums = partial[0].astype(jnp.float32)
    for d in range(1, n_kvh):
        sums = sums + exchange(partial[d], "kvh", d).astype(jnp.float32)
    return sums.astype(jnp.bfloat16)


def solution(mesh):
    placed = (
        P(None, None, "kvh"),
        P("ctx", "kvh", None, None),
        P("ctx", "kvh", None, None),
        P("kvh", "ctx"),
        P(),
        P("ctx"),
        P("ctx"),
    )
    return jax.shard_map(
        per_device, mesh=mesh, in_specs=placed, out_specs=P("kvh", "ctx"), check_vma=False
    )
```

```python
import functools
import math

import jax
import jax.numpy as jnp
from jax import lax
from jax.experimental import pallas as pl
from jax.experimental.pallas import tpu as pltpu
from jax.sharding import PartitionSpec as P

QUERY_HEADS = 64
KEY_VALUE_HEADS = 8
GROUP = QUERY_HEADS // KEY_VALUE_HEADS
DRAFT = 16
FLOOR = -1e30
LANES = 128
CHUNK = 16
COPIES = 4


def attention_kernel(
    n_ctx, hps, tg,
    len_hbm, req_hbm, page_hbm, q_hbm, k_hbm, v_hbm, *rest,
):
    msgs = rest[:n_ctx]
    len_ref, req_ref, page_ref, q_ref, k_buf, v_buf, raw, top, acc, sems, head_sems = rest[n_ctx:]
    slots, kv_local, page_len, head = k_hbm.shape
    requests = q_ref.shape[0]
    chunks = slots // CHUNK
    rows = GROUP * DRAFT
    scale = math.log2(math.e) / math.sqrt(head)

    def load(i, which):
        size = CHUNK // COPIES
        at = pl.ds(i * size, size)
        source, target = ((k_hbm, k_buf), (v_hbm, v_buf))[which]
        return pltpu.make_async_copy(source.at[at], target.at[at], sems.at[which, i])

    def start(i, which):
        for c in range(COPIES):
            load(i * COPIES + c, which).start()

    def wait(i, which):
        for c in range(COPIES):
            load(i * COPIES + c, which).wait()

    first_loads = [
        pltpu.make_async_copy(source, target, head_sems.at[n])
        for n, (source, target) in enumerate(
            ((len_hbm, len_ref), (req_hbm, req_ref), (page_hbm, page_ref), (q_hbm, q_ref))
        )
    ]
    for copy in first_loads:
        copy.start()

    @pl.loop(0, chunks)
    def _(i):
        start(i, 0)

    @pl.loop(0, requests + 1)
    def _(r):
        top[r] = jnp.full(top.shape[1:], FLOOR, jnp.float32)
        acc[r] = jnp.zeros(acc.shape[1:], jnp.float32)

    for copy in first_loads:
        copy.wait()

    ones = jnp.ones((page_len, LANES), jnp.bfloat16)

    def score(first, masked):
        for u in range(CHUNK):
            s = first + u
            r = req_ref[s]
            r_in = jnp.minimum(r, requests - 1)
            for h in range(kv_local):
                q = jnp.concatenate(
                    [q_ref[r_in, :, pl.ds((h * GROUP + g) * head, head)] for g in range(GROUP)], axis=0
                )
                scores = lax.dot_general(
                    q, k_buf[s, h], (((1,), (1,)), ((), ())), preferred_element_type=jnp.float32
                )
                if masked:
                    last = len_ref[r_in] - DRAFT - page_ref[s] * page_len
                    offset = (
                        lax.broadcasted_iota(jnp.int32, (rows, page_len), 1)
                        - lax.broadcasted_iota(jnp.int32, (rows, page_len), 0) % DRAFT
                    )
                    scores = jnp.where(offset <= last, scores, FLOOR)
                scores = scores * scale
                raw[s, h] = scores
                high = functools.reduce(
                    jnp.maximum, [scores[:, i : i + LANES] for i in range(0, page_len, LANES)]
                )
                top[r, h] = jnp.maximum(top[r, h], high)

    @pl.loop(0, chunks)
    def _(i):
        start(i, 1)
        wait(i, 0)
        cut = False
        for u in range(CHUNK):
            s = i * CHUNK + u
            r = req_ref[s]
            end = page_ref[s] * page_len + page_len - 1
            cut = cut | ((r < requests) & (end > len_ref[jnp.minimum(r, requests - 1)] - DRAFT))

        @pl.when(cut)
        def _():
            score(i * CHUNK, True)

        @pl.when(jnp.logical_not(cut))
        def _():
            score(i * CHUNK, False)

    batch = math.gcd(requests, 4)

    @pl.loop(0, requests // batch)
    def _(i):
        highs = [
            (i * batch + b, h, jnp.max(top[i * batch + b, h], axis=1, keepdims=True))
            for b in range(batch)
            for h in range(kv_local)
        ]
        for r, h, high in highs:
            top[r, h] = jnp.broadcast_to(high, (rows, LANES))

    @pl.loop(0, chunks)
    def _(i):
        wait(i, 1)
        for u in range(CHUNK):
            s = i * CHUNK + u
            r = req_ref[s]
            for h in range(kv_local):
                high = top[r, h]
                weights = jnp.concatenate(
                    [
                        jnp.exp2(raw[s, h, :, i : i + LANES] - high).astype(jnp.bfloat16)
                        for i in range(0, page_len, LANES)
                    ],
                    axis=1,
                )
                acc[r, h] += jnp.dot(
                    weights,
                    jnp.concatenate([v_buf[s, h], ones], axis=1),
                    preferred_element_type=jnp.float32,
                )

    me = lax.axis_index("ctx")
    per = requests // tg
    width = hps * LANES
    group = width // 4
    lane = lax.broadcasted_iota(jnp.int32, (DRAFT, LANES), 1)
    for d in range(n_ctx):
        dest = me ^ d
        part = dest % tg
        first_head = dest // tg * hps
        tops = jnp.full((DRAFT, LANES), FLOOR, jnp.float32)
        sums = jnp.zeros((DRAFT, LANES), jnp.float32)
        for rr in range(per):
            r = part * per + rr
            for hh in range(hps):
                q_head = first_head + hh
                h, g = q_head // GROUP, q_head % GROUP
                at = pl.ds(g * DRAFT, DRAFT)
                m = top[r, h, at, :]
                l = acc[r, h, at, head:]
                o = acc[r, h, at, :head]
                msgs[d][rr * DRAFT : (rr + 1) * DRAFT, hh * LANES : (hh + 1) * LANES] = (
                    o * pl.reciprocal(jnp.where(l > 0, l, 1.0), approx=True)
                ).astype(jnp.bfloat16)
                t = rr * hps + hh
                tops = jnp.where(lane == t, m, tops)
                sums = jnp.where(lane == t, l, sums)
        tops_sent = tops.astype(jnp.bfloat16).astype(jnp.float32)
        sums = jnp.where(tops > 0.1 * scale * FLOOR, sums * jnp.exp2(tops - tops_sent), 0.0)
        sums_high = sums.astype(jnp.bfloat16).astype(jnp.float32)
        msgs[d][per * DRAFT :, :] = jnp.concatenate(
            [x[:, :group] for x in (tops_sent, sums_high, sums - sums_high, sums)], axis=1
        ).astype(jnp.bfloat16)


def combine_kernel(final, scale, *refs):
    parts, out = refs[:-1], refs[-1]
    width = out.shape[1]
    rows = parts[0].shape[0] - DRAFT
    per, hps, group = rows // DRAFT, width // LANES, width // 4
    tops, masses = [], []
    for p in parts:
        stat = p[rows:, :].astype(jnp.float32)
        tops.append(stat[:, :group])
        masses.append(stat[:, group : 2 * group] + stat[:, 2 * group : 3 * group])
    best = functools.reduce(jnp.maximum, tops)
    shares = [l * jnp.exp2(m - best) for m, l in zip(tops, masses)]
    total = functools.reduce(jnp.add, shares)
    inverse = 1.0 / jnp.where(total > 0, total, 1.0)
    shares = [s * inverse for s in shares]
    for rr in range(per):
        for hh in range(hps):
            t = rr * hps + hh
            at = (slice(rr * DRAFT, (rr + 1) * DRAFT), slice(hh * LANES, (hh + 1) * LANES))
            out[at] = functools.reduce(
                jnp.add,
                [s[:, t : t + 1] * p[at].astype(jnp.float32) for s, p in zip(shares, parts)],
            ).astype(jnp.bfloat16)
    if not final:
        high = total.astype(jnp.bfloat16).astype(jnp.float32)
        out[rows:, :] = jnp.concatenate([best, high, total - high, total], axis=1).astype(jnp.bfloat16)


def project_kernel(order, n_kvh, tg, *refs):
    n_ctx = len(order)
    parts, w_ref = refs[:n_ctx], refs[n_ctx]
    outs = refs[n_ctx + 1 : n_ctx + 1 + n_kvh]
    a_buf, total = refs[n_ctx + 1 + n_kvh :]
    rows, width = parts[0].shape
    me = lax.axis_index("ctx")
    for d, p in zip(order, parts):
        source = me ^ d
        a_buf[
            pl.ds(pl.multiple_of(source % tg * rows, rows), rows),
            pl.ds(pl.multiple_of(source // tg * width, width), width),
        ] = p[...]
    total[...] = jnp.dot(a_buf[...], w_ref[...], preferred_element_type=jnp.float32)
    mine = lax.axis_index("kvh")
    count = outs[0].shape[0]
    for d, o in enumerate(outs):
        o[...] = total[pl.ds(pl.multiple_of((mine ^ d) * count, 8), count), :].astype(jnp.bfloat16)


def exchange(x, axis, d):
    return lax.ppermute(x, axis, [(i, i ^ d) for i in range(lax.axis_size(axis))])


def per_device(queries, keys, values, out_weight, lengths, slot_request, slot_page):
    n_ctx, n_kvh = lax.axis_size("ctx"), lax.axis_size("kvh")
    requests = queries.shape[0]
    slots, kv_local, page_len, head = keys.shape
    heads = kv_local * GROUP
    hps, tg = max(heads // n_ctx, 1), max(n_ctx // heads, 1)
    tokens = requests * DRAFT
    rows, width = tokens // tg, hps * head
    unit = GROUP * DRAFT
    smem = pl.BlockSpec(memory_space=pltpu.SMEM)
    vmem = pl.BlockSpec(memory_space=pltpu.VMEM)
    hbm = pl.BlockSpec(memory_space=pltpu.HBM)
    params = pltpu.CompilerParams(vmem_limit_bytes=46 * 2**20)
    small = pltpu.CompilerParams(vmem_limit_bytes=16 * 2**20)
    msgs = pl.pallas_call(
        functools.partial(attention_kernel, n_ctx, hps, tg),
        out_shape=[jax.ShapeDtypeStruct((rows + DRAFT, width), jnp.bfloat16)] * n_ctx,
        in_specs=[hbm] * 6,
        out_specs=[vmem] * n_ctx,
        scratch_shapes=[
            pltpu.SMEM(lengths.shape, jnp.int32),
            pltpu.SMEM(slot_request.shape, jnp.int32),
            pltpu.SMEM(slot_page.shape, jnp.int32),
            pltpu.VMEM(queries.shape, queries.dtype),
            pltpu.VMEM(keys.shape, keys.dtype),
            pltpu.VMEM(values.shape, values.dtype),
            pltpu.VMEM((slots, kv_local, unit, page_len), jnp.float32),
            pltpu.VMEM((requests + 1, kv_local, unit, LANES), jnp.float32),
            pltpu.VMEM((requests + 1, kv_local, unit, head + LANES), jnp.float32),
            pltpu.SemaphoreType.DMA((2, slots // CHUNK * COPIES)),
            pltpu.SemaphoreType.DMA((4,)),
        ],
        compiler_params=params,
    )(*(pltpu.with_memory_space_constraint(x, pltpu.HBM) for x in (lengths, slot_request, slot_page, queries)), keys, values)
    scale = math.log2(math.e) / math.sqrt(head)

    def combine(parts, final):
        shape = (rows if final else rows + DRAFT, width)
        return pl.pallas_call(
            functools.partial(combine_kernel, final, scale),
            out_shape=jax.ShapeDtypeStruct(shape, jnp.bfloat16),
            in_specs=[vmem] * len(parts),
            out_specs=vmem,
            compiler_params=small,
        )(*parts)

    near = [d for d in (2,) if d < n_ctx]
    far = sorted(range(4, n_ctx, 2))
    straight = [1, *near, *(d + 1 for d in near)]
    beside = {d: exchange(msgs[d + 1], "ctx", 1) for d in far}
    merged = [combine([msgs[d], beside[d]], False) for d in far]
    msgs = dict(enumerate(msgs))
    late = straight[1:]
    if late and far:
        held = lax.optimization_barrier((*(msgs[d] for d in late), merged[-1]))
        msgs.update(zip(late, held))
    got = [exchange(msgs[d], "ctx", d) for d in straight]
    got += [exchange(m, "ctx", d) for m, d in zip(merged, far)]
    attended = combine([msgs[0], *got], True)
    every = {d: exchange(attended, "ctx", d) for d in [*straight, *far]}
    for d in far:
        every[d + 1] = exchange(every[d], "ctx", 1)
    every[0] = attended
    order = [0, *straight, *(d + side for d in reversed(far) for side in (0, 1))]
    columns = out_weight.shape[1]
    partial = pl.pallas_call(
        functools.partial(project_kernel, order, n_kvh, tg),
        out_shape=[jax.ShapeDtypeStruct((tokens // n_kvh, columns), jnp.bfloat16)] * n_kvh,
        in_specs=[vmem] * (n_ctx + 1),
        out_specs=[vmem] * n_kvh,
        scratch_shapes=[
            pltpu.VMEM((tokens, heads * head), jnp.bfloat16),
            pltpu.VMEM((tokens, columns), jnp.float32),
        ],
        compiler_params=small,
    )(*(every[d] for d in order), out_weight)
    sums = partial[0].astype(jnp.float32)
    for d in range(1, n_kvh):
        sums = sums + exchange(partial[d], "kvh", d).astype(jnp.float32)
    return sums.astype(jnp.bfloat16)


def solution(mesh):
    placed = (
        P(None, None, "kvh"),
        P("ctx", "kvh", None, None),
        P("ctx", "kvh", None, None),
        P("kvh", "ctx"),
        P(),
        P("ctx"),
        P("ctx"),
    )
    return jax.shard_map(
        per_device, mesh=mesh, in_specs=placed, out_specs=P("kvh", "ctx"), check_vma=False
    )
```

```python
import functools
import math

import jax
import jax.numpy as jnp
from jax import lax
from jax.experimental import pallas as pl
from jax.experimental.pallas import tpu as pltpu
from jax.sharding import PartitionSpec as P

QUERY_HEADS = 64
KEY_VALUE_HEADS = 8
GROUP = QUERY_HEADS // KEY_VALUE_HEADS
DRAFT = 16
FLOOR = -1e30
LANES = 128
CHUNK = 16
COPIES = 4


def attention_kernel(
    n_ctx, hps, tg,
    len_hbm, req_hbm, page_hbm, q_hbm, k_hbm, v_hbm, *rest,
):
    msgs = rest[:n_ctx]
    len_ref, req_ref, page_ref, q_ref, k_buf, v_buf, raw, top, acc, sems, head_sems = rest[n_ctx:]
    slots, kv_local, page_len, head = k_hbm.shape
    requests = q_ref.shape[0]
    chunks = slots // CHUNK
    rows = GROUP * DRAFT
    scale = math.log2(math.e) / math.sqrt(head)

    def load(i, which):
        size = CHUNK // COPIES
        at = pl.ds(i * size, size)
        source, target = ((k_hbm, k_buf), (v_hbm, v_buf))[which]
        return pltpu.make_async_copy(source.at[at], target.at[at], sems.at[which, i])

    def start(i, which):
        for c in range(COPIES):
            load(i * COPIES + c, which).start()

    def wait(i, which):
        for c in range(COPIES):
            load(i * COPIES + c, which).wait()

    first_loads = [
        pltpu.make_async_copy(source, target, head_sems.at[n])
        for n, (source, target) in enumerate(
            ((len_hbm, len_ref), (req_hbm, req_ref), (page_hbm, page_ref), (q_hbm, q_ref))
        )
    ]
    for copy in first_loads:
        copy.start()

    @pl.loop(0, chunks)
    def _(i):
        start(i, 0)

    @pl.loop(0, requests + 1)
    def _(r):
        top[r] = jnp.full(top.shape[1:], FLOOR, jnp.float32)
        acc[r] = jnp.zeros(acc.shape[1:], jnp.float32)

    for copy in first_loads:
        copy.wait()

    ones = jnp.ones((page_len, LANES), jnp.bfloat16)

    def score(first, masked):
        for u in range(CHUNK):
            s = first + u
            r = req_ref[s]
            r_in = jnp.minimum(r, requests - 1)
            for h in range(kv_local):
                q = jnp.concatenate(
                    [q_ref[r_in, :, pl.ds((h * GROUP + g) * head, head)] for g in range(GROUP)], axis=0
                )
                scores = lax.dot_general(
                    q, k_buf[s, h], (((1,), (1,)), ((), ())), preferred_element_type=jnp.float32
                )
                if masked:
                    last = len_ref[r_in] - DRAFT - page_ref[s] * page_len
                    offset = (
                        lax.broadcasted_iota(jnp.int32, (rows, page_len), 1)
                        - lax.broadcasted_iota(jnp.int32, (rows, page_len), 0) % DRAFT
                    )
                    scores = jnp.where(offset <= last, scores, FLOOR)
                scores = scores * scale
                raw[s, h] = scores
                high = functools.reduce(
                    jnp.maximum, [scores[:, i : i + LANES] for i in range(0, page_len, LANES)]
                )
                top[r, h] = jnp.maximum(top[r, h], high)

    @pl.loop(0, chunks)
    def _(i):
        start(i, 1)
        wait(i, 0)
        cut = False
        for u in range(CHUNK):
            s = i * CHUNK + u
            r = req_ref[s]
            end = page_ref[s] * page_len + page_len - 1
            cut = cut | ((r < requests) & (end > len_ref[jnp.minimum(r, requests - 1)] - DRAFT))

        @pl.when(cut)
        def _():
            score(i * CHUNK, True)

        @pl.when(jnp.logical_not(cut))
        def _():
            score(i * CHUNK, False)

    batch = math.gcd(requests, 4)

    @pl.loop(0, requests // batch)
    def _(i):
        highs = [
            (i * batch + b, h, jnp.max(top[i * batch + b, h], axis=1, keepdims=True))
            for b in range(batch)
            for h in range(kv_local)
        ]
        for r, h, high in highs:
            top[r, h] = jnp.broadcast_to(high, (rows, LANES))

    @pl.loop(0, chunks)
    def _(i):
        wait(i, 1)
        for u in range(CHUNK):
            s = i * CHUNK + u
            r = req_ref[s]
            for h in range(kv_local):
                high = top[r, h]
                weights = jnp.concatenate(
                    [
                        jnp.exp2(raw[s, h, :, i : i + LANES] - high).astype(jnp.bfloat16)
                        for i in range(0, page_len, LANES)
                    ],
                    axis=1,
                )
                acc[r, h] += jnp.dot(
                    weights,
                    jnp.concatenate([v_buf[s, h], ones], axis=1),
                    preferred_element_type=jnp.float32,
                )

    me = lax.axis_index("ctx")
    per = requests // tg
    width = hps * LANES
    group = width // 4
    lane = lax.broadcasted_iota(jnp.int32, (DRAFT, LANES), 1)
    for d in range(n_ctx):
        dest = me ^ d
        part = dest % tg
        first_head = dest // tg * hps
        tops = jnp.full((DRAFT, LANES), FLOOR, jnp.float32)
        sums = jnp.zeros((DRAFT, LANES), jnp.float32)
        for rr in range(per):
            r = part * per + rr
            for hh in range(hps):
                q_head = first_head + hh
                h, g = q_head // GROUP, q_head % GROUP
                at = pl.ds(g * DRAFT, DRAFT)
                m = top[r, h, at, :]
                l = acc[r, h, at, head:]
                o = acc[r, h, at, :head]
                msgs[d][rr * DRAFT : (rr + 1) * DRAFT, hh * LANES : (hh + 1) * LANES] = (
                    o * pl.reciprocal(jnp.where(l > 0, l, 1.0), approx=True)
                ).astype(jnp.bfloat16)
                t = rr * hps + hh
                tops = jnp.where(lane == t, m, tops)
                sums = jnp.where(lane == t, l, sums)
        tops_sent = tops.astype(jnp.bfloat16).astype(jnp.float32)
        sums = jnp.where(tops > 0.1 * scale * FLOOR, sums * jnp.exp2(tops - tops_sent), 0.0)
        sums_high = sums.astype(jnp.bfloat16).astype(jnp.float32)
        msgs[d][per * DRAFT :, :] = jnp.concatenate(
            [x[:, :group] for x in (tops_sent, sums_high, sums - sums_high, sums)], axis=1
        ).astype(jnp.bfloat16)


def combine_kernel(final, scale, *refs):
    parts, out = refs[:-1], refs[-1]
    width = out.shape[1]
    rows = parts[0].shape[0] - DRAFT
    per, hps, group = rows // DRAFT, width // LANES, width // 4
    tops, masses = [], []
    for p in parts:
        stat = p[rows:, :].astype(jnp.float32)
        tops.append(stat[:, :group])
        masses.append(stat[:, group : 2 * group] + stat[:, 2 * group : 3 * group])
    best = functools.reduce(jnp.maximum, tops)
    shares = [l * jnp.exp2(m - best) for m, l in zip(tops, masses)]
    total = functools.reduce(jnp.add, shares)
    inverse = 1.0 / jnp.where(total > 0, total, 1.0)
    shares = [s * inverse for s in shares]
    for rr in range(per):
        for hh in range(hps):
            t = rr * hps + hh
            at = (slice(rr * DRAFT, (rr + 1) * DRAFT), slice(hh * LANES, (hh + 1) * LANES))
            out[at] = functools.reduce(
                jnp.add,
                [s[:, t : t + 1] * p[at].astype(jnp.float32) for s, p in zip(shares, parts)],
            ).astype(jnp.bfloat16)
    if not final:
        high = total.astype(jnp.bfloat16).astype(jnp.float32)
        out[rows:, :] = jnp.concatenate([best, high, total - high, total], axis=1).astype(jnp.bfloat16)


def project_kernel(order, n_kvh, tg, first, last, *refs):
    refs = list(refs)
    before = None if first else refs.pop(0)
    parts = [refs.pop(0) for _ in order]
    w_ref = refs.pop(0)
    columns = w_ref.shape[1]
    rows, width = parts[0].shape
    me = lax.axis_index("ctx")
    if tg == 1:
        a_buf, w_buf = None, [
            w_ref.at[pl.ds(pl.multiple_of((me ^ d) * width, width), width)] for d in order
        ]
    else:
        a_buf = refs.pop()
        for d, p in zip(order, parts):
            source = me ^ d
            a_buf[
                pl.ds(pl.multiple_of(source % tg * rows, rows), rows),
                pl.ds(pl.multiple_of(source // tg * width, width), width),
            ] = p[...]
        parts, w_buf = [a_buf], [w_ref]
    total = refs.pop()
    step = math.gcd(columns, 256)
    for c in range(0, columns, step):
        at = slice(c, c + step)
        sums = [jnp.dot(p[...], w[:, at], preferred_element_type=jnp.float32) for p, w in zip(parts, w_buf)]
        if before is not None:
            sums.append(before[:, at])
        total[:, at] = functools.reduce(jnp.add, sums)
    if last:
        mine = lax.axis_index("kvh")
        count = refs[0].shape[0]
        for d, o in enumerate(refs):
            o[...] = total[pl.ds(pl.multiple_of((mine ^ d) * count, 8), count), :].astype(jnp.bfloat16)


def exchange(x, axis, d):
    return lax.ppermute(x, axis, [(i, i ^ d) for i in range(lax.axis_size(axis))])


def per_device(queries, keys, values, out_weight, lengths, slot_request, slot_page):
    n_ctx, n_kvh = lax.axis_size("ctx"), lax.axis_size("kvh")
    requests = queries.shape[0]
    slots, kv_local, page_len, head = keys.shape
    heads = kv_local * GROUP
    hps, tg = max(heads // n_ctx, 1), max(n_ctx // heads, 1)
    tokens = requests * DRAFT
    rows, width = tokens // tg, hps * head
    unit = GROUP * DRAFT
    smem = pl.BlockSpec(memory_space=pltpu.SMEM)
    vmem = pl.BlockSpec(memory_space=pltpu.VMEM)
    hbm = pl.BlockSpec(memory_space=pltpu.HBM)
    params = pltpu.CompilerParams(vmem_limit_bytes=46 * 2**20)
    small = pltpu.CompilerParams(vmem_limit_bytes=16 * 2**20)
    msgs = pl.pallas_call(
        functools.partial(attention_kernel, n_ctx, hps, tg),
        out_shape=[jax.ShapeDtypeStruct((rows + DRAFT, width), jnp.bfloat16)] * n_ctx,
        in_specs=[hbm] * 6,
        out_specs=[vmem] * n_ctx,
        scratch_shapes=[
            pltpu.SMEM(lengths.shape, jnp.int32),
            pltpu.SMEM(slot_request.shape, jnp.int32),
            pltpu.SMEM(slot_page.shape, jnp.int32),
            pltpu.VMEM(queries.shape, queries.dtype),
            pltpu.VMEM(keys.shape, keys.dtype),
            pltpu.VMEM(values.shape, values.dtype),
            pltpu.VMEM((slots, kv_local, unit, page_len), jnp.float32),
            pltpu.VMEM((requests + 1, kv_local, unit, LANES), jnp.float32),
            pltpu.VMEM((requests + 1, kv_local, unit, head + LANES), jnp.float32),
            pltpu.SemaphoreType.DMA((2, slots // CHUNK * COPIES)),
            pltpu.SemaphoreType.DMA((4,)),
        ],
        compiler_params=params,
    )(*(pltpu.with_memory_space_constraint(x, pltpu.HBM) for x in (lengths, slot_request, slot_page, queries)), keys, values)
    scale = math.log2(math.e) / math.sqrt(head)

    def combine(parts, final):
        shape = (rows if final else rows + DRAFT, width)
        return pl.pallas_call(
            functools.partial(combine_kernel, final, scale),
            out_shape=jax.ShapeDtypeStruct(shape, jnp.bfloat16),
            in_specs=[vmem] * len(parts),
            out_specs=vmem,
            compiler_params=small,
        )(*parts)

    close = [d for d in (1, 2, 3) if d < n_ctx]
    distant = range(4, n_ctx, 4)
    pieces = dict(enumerate(msgs))
    merged = [
        combine([pieces[e], *(exchange(pieces[e + d], "ctx", d) for d in close)], False)
        for e in distant
    ]
    late = []
    if late and merged:
        held = lax.optimization_barrier((*(pieces[d] for d in late), *merged))
        pieces.update(zip(late, held))
    got = [exchange(pieces[d], "ctx", d) for d in close]
    got += [exchange(m, "ctx", e) for m, e in zip(merged, distant)]
    attended = combine([msgs[0], *got], True)
    near = [d for d in (2,) if d < n_ctx]
    far = sorted(range(4, n_ctx, 2))
    straight = [1, *near, *(d + 1 for d in near)]
    every = {d: exchange(attended, "ctx", d) for d in [*straight, *far]}
    for d in far:
        every[d + 1] = exchange(every[d], "ctx", 1)
    every[0] = attended
    order = [0, *straight, *(d + side for d in reversed(far) for side in (0, 1))]
    columns = out_weight.shape[1]
    tail = [d for d in order if d >= 4 and d % 2] if tg == 1 else []
    head_parts = [d for d in [0, *reversed(straight), *reversed(far)] if d not in tail]
    tail = tail[::-1]

    def project(ds, first, last, *carry):
        outs = [jax.ShapeDtypeStruct((tokens // n_kvh, columns), jnp.bfloat16)] * n_kvh
        whole = jax.ShapeDtypeStruct((tokens, columns), jnp.float32)
        scratch = [pltpu.VMEM(whole.shape, whole.dtype)] if last else []
        if tg > 1:
            scratch.append(pltpu.VMEM((tokens, heads * head), jnp.bfloat16))
        return pl.pallas_call(
            functools.partial(project_kernel, ds, n_kvh, tg, first, last),
            out_shape=outs if last else whole,
            in_specs=[vmem] * (len(carry) + len(ds) + 1),
            out_specs=[vmem] * n_kvh if last else vmem,
            scratch_shapes=scratch,
            compiler_params=small,
            cost_estimate=pl.CostEstimate(
                flops=2 * rows * width * columns * len(ds),
                bytes_accessed=2 * width * columns * len(ds),
                transcendentals=0,
            ),
        )(*carry, *(every[d] for d in ds), out_weight)

    if tail:
        partial = project(tail, False, True, project(head_parts, True, False))
    else:
        partial = project(order, True, True)
    sums = partial[0].astype(jnp.float32)
    for d in range(1, n_kvh):
        sums = sums + exchange(partial[d], "kvh", d).astype(jnp.float32)
    return sums.astype(jnp.bfloat16)


def solution(mesh):
    placed = (
        P(None, None, "kvh"),
        P("ctx", "kvh", None, None),
        P("ctx", "kvh", None, None),
        P("kvh", "ctx"),
        P(),
        P("ctx"),
        P("ctx"),
    )
    return jax.shard_map(
        per_device, mesh=mesh, in_specs=placed, out_specs=P("kvh", "ctx"), check_vma=False
    )
```
